128 devices in a mesh: src: 16 (over y_hi, z, core), frq: 8 (over y_lo, x).
Axes of the slice: x: 4, y: 4 (y_hi: 2, y_lo: 2; y = y_hi * 2 + y_lo), z: 4, core: 2. Of those that a mesh axis runs over, the one named last changes fastest.
Arguments:
- coeffs: bfloat16 [256, 2048, 2, 256], P('frq', 'src'), may hold values from -6 to 6
- angles: bfloat16 [3, 256, 2048, 256], P(None, 'frq', 'src'), may hold values from -3.140625 to 3.140625
- interp: bfloat16 [3, 2, 2, 256, 256], replicated, may hold values from -0.375 to 0.375
- pattern: int32 [3, 4, 2], replicated, may hold values from 0 to 3, all different within a row
- target_map: bfloat16 [256, 256], replicated, may hold values from -0.375 to 0.375
Outputs:
- result: float32 [256, 2048, 2, 256], P(None, ('src', 'frq'))
The draws below stay inside these ranges and needn't reach their ends.
Inputs may be any that keep to these rules, and one draw needn't show every extreme that they name: `pattern`: each row of a level names 2 different blocks, and every block is named at some level.
All inputs are finite; a program needn't handle non-finite values.
Results may differ from the reference program's by a relative error of at most 0.007.
Values may be sent and summed in bfloat16 or wider, within the bound.
No kernel may reach another device: no remote copies, remote signals or barrier semaphores. Data moves between devices by JAX's collectives and lax.ppermute only.
A program may use at most 128 MiB of HBM per device.

```python
import jax
import jax.numpy as jnp
from jax import lax

P_SIZE = 256
BLOCK = 64
NBLK = 4
KEEP = 2
LEVELS = 3
SB_DEV = 128
NF = 256
NS = 2048
N_SRC = 16


def block_levels(key, dims, shards, low, top_value):
    factor_of, own = 1.0, jax.random.fold_in(key, 6)
    for axis_at, shards_of in shards:
        steps = jnp.exp(jax.random.uniform(jax.random.fold_in(own, axis_at), (shards_of,), jnp.float32, low / len(shards), top_value / len(shards)))
        factor_of = factor_of * jnp.repeat(steps, dims[axis_at] // shards_of).reshape([-1 if axis == axis_at else 1 for axis in range(len(dims))])
    return factor_of


def choose_distinct(key, rows, number_of, top, lift):
    order = jax.random.permutation(jax.random.fold_in(key, 1), number_of)
    favour = order
    for power in range(3):
        favour = favour * favour // number_of
    favour = favour * lift // number_of
    lots = jax.random.randint(jax.random.fold_in(key, 2), (rows, number_of), 0, 4096) + favour
    fixed_rows = jax.random.permutation(jax.random.fold_in(key, 3), rows)[jnp.arange(number_of) % rows]
    lots = jnp.where(jnp.arange(rows)[:, None] == fixed_rows[None, :], 1 << 14, lots)
    score = lots * number_of + jnp.arange(number_of)
    return lax.top_k(score.astype(jnp.int32), top)[1].astype(jnp.int32)


def noise(stream_key, dims, deviation, most, shards=(), kind=jnp.bfloat16):
    level = block_levels(stream_key, dims, shards, -0.22, 0.18) if shards else 1.0
    drawn = jax.random.normal(stream_key, dims, jnp.float32) * deviation * level
    return jnp.minimum(jnp.maximum(drawn, -most), most).astype(kind)


def setup_inputs(seed: int = 0) -> dict:
    streams_of = jax.random.split(jax.random.key(seed), 6)
    return {
        "coeffs": noise(streams_of[0], (NF, NS, 2, P_SIZE), 1.0, 6.0, ((0, 8), (1, 16))),
        "angles": jnp.clip(jax.random.uniform(streams_of[1], (LEVELS, NF, NS, P_SIZE), jnp.float32, -3.140625, 3.140625), -3.140625, 3.140625).astype(jnp.bfloat16),
        "interp": noise(streams_of[2], (LEVELS, 2, 2, P_SIZE, P_SIZE), P_SIZE ** -0.5, 0.375),
        "pattern": choose_distinct(streams_of[3], LEVELS * NBLK, NBLK, KEEP, 0).reshape((LEVELS, NBLK, KEEP)),
        "target_map": noise(streams_of[4], (NF, NF), NF ** -0.5, 0.375),
    }


def block_mask(pattern_row):
    blocks = pattern_row.shape[0]
    small = jnp.any(pattern_row[:, :, None] == jnp.arange(blocks, dtype=jnp.int32)[None, None, :], axis=1)
    return jnp.repeat(jnp.repeat(small.T, BLOCK, axis=0), BLOCK, axis=1)


def rotate(current, phases):
    angle_f = phases.astype(jnp.float32)
    cos_part = jnp.cos(angle_f)
    sin_part = jnp.sin(angle_f)
    real_part = current[:, :, 0].astype(jnp.float32)
    imag_part = current[:, :, 1].astype(jnp.float32)
    turned = jnp.stack([real_part * cos_part - imag_part * sin_part, real_part * sin_part + imag_part * cos_part], axis=2)
    return turned.astype(jnp.bfloat16)


def reference(coeffs, angles, interp, pattern, target_map):
    current = coeffs
    for height in range(LEVELS):
        rotated = rotate(current, angles[height]).astype(jnp.float32)
        masked = jnp.where(block_mask(pattern[height])[None, None], interp[height].astype(jnp.float32), jnp.float32(0.0))
        span = 1 << height
        shaped = rotated.reshape(NF, N_SRC // (2 * span), 2, span, SB_DEV, 2, P_SIZE)
        mixed = jnp.einsum('fahescp,bhpq->fabescq', shaped, masked)
        current = mixed.reshape(NF, NS, 2, P_SIZE).astype(jnp.bfloat16)
    return jnp.einsum('gf,fscp->gscp', target_map.astype(jnp.float32), current.astype(jnp.float32))
```

```python
import functools

import jax
import jax.numpy as jnp
import numpy as np
from jax import lax
from jax.experimental import pallas as pl
from jax.experimental.pallas import tpu as pltpu
from jax.sharding import PartitionSpec as P

BLOCK = 64
LEVELS = 3
CHUNKS = (4, 4, 4, 4)
STEP = 2
SB = 128
W = 256
BF = jnp.bfloat16
F32 = jnp.float32

_x = np.cos((np.arange(400) + 0.5) * np.pi / 400) * 3.1410
_u = (_x * _x) / 10.0
COS = np.linalg.lstsq(np.stack([_u**k for k in range(6)], 1), np.cos(_x), rcond=None)[0]
SIN = np.linalg.lstsq(np.stack([_x * _u**k for k in range(5)], 1), np.sin(_x), rcond=None)[0]
COS = [float(c / 10.0**k) for k, c in enumerate(COS)]
SIN = [float(c / 10.0**k) for k, c in enumerate(SIN)]


def cos_sin(x):
    u = x * x
    c = COS[5] * u + COS[4]
    for k in (3, 2, 1, 0):
        c = c * u + COS[k]
    s = SIN[4] * u + SIN[3]
    for k in (2, 1, 0):
        s = s * u + SIN[k]
    return c, s * x


def turn(re, im, angle):
    c, s = cos_sin(angle.astype(F32))
    return (re * c - im * s).astype(BF), (re * s + im * c).astype(BF)


def dot(a, b):
    return jnp.dot(a, b, preferred_element_type=F32)


def call(kernel, name, grid, in_specs, out_specs, out_shape, prefetch=0, scratch=(), flops=0, nbytes=0):
    return pl.pallas_call(
        kernel,
        out_shape=out_shape,
        grid_spec=pltpu.PrefetchScalarGridSpec(
            num_scalar_prefetch=prefetch, grid=grid, in_specs=in_specs, out_specs=out_specs, scratch_shapes=list(scratch)
        ),
        compiler_params=pltpu.CompilerParams(vmem_limit_bytes=40 << 20),
        cost_estimate=pl.CostEstimate(flops=int(flops), bytes_accessed=int(nbytes), transcendentals=0),
        name=name,
    )


def weights_kernel(meta, pattern, interp, out):
    t = pl.program_id(0)
    slot = t // 2
    level = jnp.where(slot < 2, 1, jnp.where(slot == 2, 0, 2))
    rows = lax.broadcasted_iota(jnp.int32, (W, W), 0) // BLOCK
    cols = lax.broadcasted_iota(jnp.int32, (W, W), 1) // BLOCK
    keep = None
    for q in range(4):
        for k in range(2):
            hit = (cols == q) & (rows == pattern[level * 8 + q * 2 + k])
            keep = hit if keep is None else keep | hit
    w = interp[0, 0, 0].astype(F32)
    out[0] = jnp.where(keep, w, jnp.zeros_like(w)).astype(BF)


def weights(meta, pattern, interp):
    def pick(t, meta, pattern):
        slot = t // 2
        level = jnp.where(slot < 2, 1, jnp.where(slot == 2, 0, 2))
        bit = meta[level]
        return level, bit ^ jnp.where(slot == 1, 1, 0), bit ^ (t & 1), 0, 0

    return call(
        weights_kernel, "masked_weights", (8,),
        [pl.BlockSpec((1, 1, 1, W, W), pick)],
        pl.BlockSpec((1, W, W), lambda t, *_: (t // 2, t % 2, 0)),
        jax.ShapeDtypeStruct((4, 2 * W, W), BF), prefetch=2, flops=0, nbytes=2 << 20,
    )(meta, pattern, interp)


def first_kernel(shuffle, coeffs, angles, out):
    for a in range(2):
        for i in range(STEP):
            x = jnp.concatenate([coeffs[a, i, : 2 * SB], coeffs[a, i, 2 * SB :]], axis=1)
            y = dot(shuffle[...], x)
            for part in range(2):
                lanes = slice(part * 128, part * 128 + 128)
                for r in range(0, 64, 32):
                    row = [y[k * 64 + r : k * 64 + r + 32, lanes] for k in range(4)]
                    at = part * 64 + r
                    re, im = turn(
                        jnp.concatenate(row[:2], axis=1), jnp.concatenate(row[2:], axis=1), angles[0, a, i, at : at + 32]
                    )
                    out[a, i, at : at + 32, :W] = re
                    out[a, i, at : at + 32, W:] = im


def first(shuffle, coeffs, angles, off, n):
    return call(
        first_kernel, "rotate_0", (n // STEP,),
        [
            pl.BlockSpec((W, W), lambda t: (0, 0)),
            pl.BlockSpec((2, STEP, 4 * SB, 128), lambda t: (0, off // STEP + t, 0, 0)),
            pl.BlockSpec((1, 2, STEP, SB, W), lambda t: (0, 0, off // STEP + t, 0, 0)),
        ],
        pl.BlockSpec((2, STEP, SB, 2 * W), lambda t: (0, t, 0, 0)),
        jax.ShapeDtypeStruct((2, n, SB, 2 * W), BF), flops=n * 2e8, nbytes=n * 700e3,
    )(shuffle, coeffs, angles)


def sides(own, other):
    return jnp.concatenate(
        [jnp.concatenate([own[:, :W], other[:, :W]], axis=1), jnp.concatenate([own[:, W:], other[:, W:]], axis=1)], axis=0
    )


def turn_rows(y, angles, store):
    for r in range(0, SB, 32):
        re, im = turn(y[r : r + 32], y[SB + r : SB + r + 32], angles[r : r + 32])
        store(r, re, im)


def second_kernel(meta, own, other, w, angles, keep, send):
    h = meta[3]
    for out, a in ((send, 1 - h), (keep, h)):
        for i in range(STEP):
            y = dot(sides(own[a, i], other[a, i]), w[0])

            def store(r, re, im, out=out, i=i):
                out[i, r : r + 32, :W] = re
                out[i, r : r + 32, W:] = im

            turn_rows(y, angles.at[0, a, i], store)


def second(meta, own, other, w, angles, off, n):
    both = pl.BlockSpec((2, STEP, SB, 2 * W), lambda t, *_: (0, t, 0, 0))
    one = pl.BlockSpec((STEP, SB, 2 * W), lambda t, *_: (t, 0, 0))
    return call(
        second_kernel, "mix_0_rotate_1", (n // STEP,),
        [
            both,
            both,
            pl.BlockSpec((1, 2 * W, W), lambda t, *_: (2, 0, 0)),
            pl.BlockSpec((1, 2, STEP, SB, W), lambda t, *_: (1, 0, off // STEP + t, 0, 0)),
        ],
        [one, one],
        [jax.ShapeDtypeStruct((n, SB, 2 * W), BF)] * 2, prefetch=1, flops=n * 2e8, nbytes=n * 1e6,
    )(meta, own, other, w, angles)


def third_kernel(meta, own, other, w, angles, angles_other, out):
    for i in range(STEP):
        x = sides(own[i], other[i])
        for g, angle in ((0, angles.at[0, 0, i]), (1, angles_other.at[i])):
            y = dot(x, w[g])

            def store(r, re, im, g=g, i=i):
                out[g, i, r : r + 32, :W] = re
                out[g, i, r : r + 32, W:] = im

            turn_rows(y, angle, store)


def third(meta, own, other, w, angles, angles_other, off, n):
    one = pl.BlockSpec((STEP, SB, 2 * W), lambda t, *_: (t, 0, 0))
    return call(
        third_kernel, "mix_1_rotate_2", (n // STEP,),
        [
            one,
            one,
            pl.BlockSpec((2, 2 * W, W), lambda t, *_: (0, 0, 0)),
            pl.BlockSpec((1, 1, STEP, SB, W), lambda t, meta: (2, meta[3], off // STEP + t, 0, 0)),
            pl.BlockSpec((STEP, SB, W), lambda t, *_: (off // STEP + t, 0, 0)),
        ],
        pl.BlockSpec((2, STEP, SB, 2 * W), lambda t, *_: (0, t, 0, 0)),
        jax.ShapeDtypeStruct((2, n, SB, 2 * W), BF), prefetch=1, flops=n * 2e8, nbytes=n * 700e3,
    )(meta, own, other, w, angles, angles_other)


def back_kernel(own, other, w, out):
    for i in range(STEP):
        y = dot(sides(own[0, i], other[0, i]), w[0])
        out[i, :, :W] = y[:SB].astype(BF)
        out[i, :, W:] = y[SB:].astype(BF)


def back(own, other, w, n):
    return call(
        back_kernel, "mix_2_other", (n // STEP,),
        [
            pl.BlockSpec((1, STEP, SB, 2 * W), lambda t: (1, t, 0, 0)),
            pl.BlockSpec((1, STEP, SB, 2 * W), lambda t: (0, t, 0, 0)),
            pl.BlockSpec((1, 2 * W, W), lambda t: (3, 0, 0)),
        ],
        pl.BlockSpec((STEP, SB, 2 * W), lambda t: (t, 0, 0)),
        jax.ShapeDtypeStruct((n, SB, 2 * W), BF), flops=n * 1e8, nbytes=n * 400e3,
    )(own, other, w)


def split_kernel(meta, own, other, w, came, *outs_scratch):
    outs, held = outs_scratch[:8], outs_scratch[8]
    q = meta[4]
    for i in range(STEP):
        y = dot(sides(own[0, i], other[0, i]), w[0])
        held[i, :, :W] = y[:SB].astype(BF)
        held[i, :, W:] = y[SB:].astype(BF)
    for m in range(8):
        at = pl.ds(pl.multiple_of((q ^ m) * 16, 16), 16)
        for i in range(STEP):
            outs[m][0, i] = held[i, at, :]
            outs[m][1, i] = came[i, at, :]


def split(meta, own, other, w, came, n):
    return call(
        split_kernel, "mix_2_own_split", (n // STEP,),
        [
            pl.BlockSpec((1, STEP, SB, 2 * W), lambda t, *_: (0, t, 0, 0)),
            pl.BlockSpec((1, STEP, SB, 2 * W), lambda t, *_: (1, t, 0, 0)),
            pl.BlockSpec((1, 2 * W, W), lambda t, *_: (3, 0, 0)),
            pl.BlockSpec((STEP, SB, 2 * W), lambda t, *_: (t, 0, 0)),
        ],
        [pl.BlockSpec((2, STEP, 16, 2 * W), lambda t, *_: (0, t, 0, 0))] * 8,
        [jax.ShapeDtypeStruct((2, n, 16, 2 * W), BF)] * 8, prefetch=1,
        scratch=[pltpu.VMEM((STEP, SB, 2 * W), BF)], flops=n * 1e8, nbytes=n * 800e3,
    )(meta, own, other, w, came)


def gather_kernel(n, shuffle, *refs):
    pieces, out = refs[:8], refs[8]
    per = 16 // (2 * n)
    for group in range(8 // per):
        rows = []
        for m in range(group * per, group * per + per):
            for half in range(2):
                for i in range(n):
                    rows.append(pieces[m][half, i])
        y = dot(shuffle[...], jnp.concatenate(rows, axis=0)).astype(BF)
        for j in range(16):
            out[j, group * 16 : group * 16 + 16, :] = y[j * 16 : j * 16 + 16]


def gather(shuffle, pieces, n):
    return call(
        functools.partial(gather_kernel, n), "gather_frequencies", (1,),
        [pl.BlockSpec((W, W), lambda t: (0, 0))] + [pl.BlockSpec((2, n, 16, 2 * W), lambda t: (0, 0, 0, 0))] * 8,
        pl.BlockSpec((16, 16 * n, 2 * W), lambda t: (0, 0, 0)),
        jax.ShapeDtypeStruct((16, 16 * n, 2 * W), BF), flops=n * 1e8, nbytes=n * 500e3,
    )(shuffle, *pieces)


def target_kernel(chunks, t_map, *refs):
    parts, out = refs[:chunks], refs[chunks]
    for j in range(2):
        y = dot(t_map[...], jnp.concatenate([p[j] for p in parts], axis=0))
        for c in range(2):
            for half in range(2):
                at = c * W + half * 128
                out[:, j * 4 + half * 2 + c, :] = y[:, at : at + 128]


def target(t_map, parts):
    return call(
        functools.partial(target_kernel, len(parts)), "target_map", (8,),
        [pl.BlockSpec((W, W), lambda t: (0, 0))]
        + [pl.BlockSpec((2, p.shape[1], 2 * W), lambda t: (t, 0, 0)) for p in parts],
        pl.BlockSpec((W, 8, 128), lambda t: (0, t, 0)),
        jax.ShapeDtypeStruct((W, 64, 128), F32), flops=1e9, nbytes=12 << 20,
    )(t_map, *parts)


def swap(value, axis, mask):
    return lax.ppermute(value, axis, [(i, i ^ mask) for i in range(lax.axis_size(axis))])


def shuffles():
    first_rows = np.zeros((W, W), np.float32)
    last_rows = np.zeros((W, W), np.float32)
    for j in range(64):
        for half in range(2):
            for c in range(2):
                first_rows[(c * 2 + half) * 64 + j, j * 4 + half * 2 + c] = 1
    for j in range(16):
        for f in range(16):
            last_rows[j * 16 + f, f * 16 + j] = 1
    return jnp.asarray(first_rows, BF), jnp.asarray(last_rows, BF)


def on_device(coeffs, angles, interp, pattern, target_map):
    src, frq = lax.axis_index("src"), lax.axis_index("frq")
    bits = [src >> k & 1 for k in range(LEVELS)]
    h = bits[1] ^ bits[2]
    meta = jnp.stack([*bits, h, frq]).astype(jnp.int32)
    spread, close = shuffles()
    coeffs = coeffs.reshape(2, 16, SB, 2, 2, 128).transpose(0, 1, 2, 4, 3, 5).reshape(2, 16, 4 * SB, 128)
    angles = angles.reshape(LEVELS, 2, 16, SB, W)

    offs = np.cumsum((0,) + CHUNKS)[:-1].tolist()
    order = np.concatenate(
        [
            np.asarray([m << 5 | half << 4 | off + i for m in range(8) for half in range(2) for i in range(n)])
            for off, n in zip(offs, CHUNKS)
        ]
    )
    chosen = jnp.asarray(order, jnp.int32) ^ (frq << 5) ^ (h << 4)
    hot = (jnp.arange(W, dtype=jnp.int32)[:, None] == chosen[None, :]).astype(BF)
    t_map = jnp.dot(target_map, hot, preferred_element_type=F32).astype(BF)

    angles_other = swap(lax.dynamic_index_in_dim(angles[2], 1 - h, 0, keepdims=False), "src", 2)
    w = weights(meta, pattern.reshape(-1), interp)
    parts = []
    for off, n in zip(offs, CHUNKS):
        turned = first(spread, coeffs, angles, off, n)
        keep, send = second(meta, turned, swap(turned, "src", 1), w, angles, off, n)
        turned = third(meta, keep, swap(send, "src", 2), w, angles, angles_other, off, n)
        other = swap(turned, "src", 6)
        came = swap(back(turned, other, w, n), "src", 2)
        pieces = split(meta, turned, other, w, came, n)
        pieces = [pieces[0]] + [swap(pieces[m], "frq", m) for m in range(1, 8)]
        parts.append(gather(close, pieces, n))
    out = target(t_map, parts)
    return out.reshape(W, 16, 2, 2, 128).transpose(0, 1, 3, 2, 4).reshape(W, 16, 2, W)


def solution(mesh):
    return jax.shard_map(
        on_device,
        mesh=mesh,
        in_specs=(P("frq", "src", None, None), P(None, "frq", "src", None), P(), P(), P()),
        out_specs=P(None, ("src", "frq"), None, None),
        check_vma=False,
    )
```

```python
import functools

import jax
import jax.numpy as jnp
import numpy as np
from jax import lax
from jax.experimental import pallas as pl
from jax.experimental.pallas import tpu as pltpu
from jax.sharding import PartitionSpec as P

BLOCK = 64
LEVELS = 3
CHUNKS = (4, 4, 4, 4)
STEPS = (
    "F0", "W0", "F1", "S0", "F2", "S1", "F3", "S2", "T0", "S3", "T1", "B0",
    "T2", "B1", "X0", "T3", "B2", "X1", "B3", "X2", "G0", "X3", "G1", "G2",
    "G3",
)
AFTER = {"W0": ("F0",), "F1": ("W0",), "S0": ("F1",), "F2": ("S0",), "S1": ("F2",), "F3": ("S1",), "S2": ("F3",), "T0": ("S2",), "S3": ("T0",), "T1": ("S3",), "B0": ("T1",), "T2": ("B0",), "B1": ("T2",), "X0": ("B1",), "T3": ("X0",), "B2": ("T3",), "X1": ("B2",), "B3": ("X1",), "X2": ("B3",), "G0": ("X2",), "X3": ("G0",), "G1": ("X3",), "G2": ("G1",), "G3": ("G2",)}
STEP = 2
FIRST_LIMIT = 60
LIMIT = 40
COST = 20.0
SB = 128
W = 256
BF = jnp.bfloat16
F32 = jnp.float32

_x = np.cos((np.arange(400) + 0.5) * np.pi / 400) * 3.1410
_u = (_x * _x) / 10.0
COS = np.linalg.lstsq(np.stack([_u**k for k in range(6)], 1), np.cos(_x), rcond=None)[0]
SIN = np.linalg.lstsq(np.stack([_x * _u**k for k in range(5)], 1), np.sin(_x), rcond=None)[0]
COS = [float(c / 10.0**k) for k, c in enumerate(COS)]
SIN = [float(c / 10.0**k) for k, c in enumerate(SIN)]


def cos_sin(x):
    u = x * x
    c = COS[5] * u + COS[4]
    for k in (3, 2, 1, 0):
        c = c * u + COS[k]
    s = SIN[4] * u + SIN[3]
    for k in (2, 1, 0):
        s = s * u + SIN[k]
    return c, s * x


def turn(re, im, angle):
    c, s = cos_sin(angle.astype(F32))
    return (re * c - im * s).astype(BF), (re * s + im * c).astype(BF)


def dot(a, b):
    return jnp.dot(a, b, preferred_element_type=F32)


class Order:
    def __init__(self):
        self.last = []

    def __call__(self, kernel, name, grid, in_specs, out_specs, out_shape, prefetch=0, scratch=(), flops=0, nbytes=0, limit=None):
        at = prefetch + len(in_specs)

        def body(*refs):
            kernel(*refs[:at], *refs[at + len(before) :])

        before = list(self.last)
        run = pl.pallas_call(
            body,
            out_shape=out_shape,
            grid_spec=pltpu.PrefetchScalarGridSpec(
                num_scalar_prefetch=prefetch,
                grid=grid,
                in_specs=list(in_specs) + [pl.BlockSpec(memory_space=pl.ANY)] * len(before),
                out_specs=out_specs,
                scratch_shapes=list(scratch),
            ),
            compiler_params=pltpu.CompilerParams(vmem_limit_bytes=(limit or LIMIT) << 20),
            cost_estimate=pl.CostEstimate(flops=int(flops * COST), bytes_accessed=int(nbytes * COST), transcendentals=0),
            name=name,
        )

        def go(*operands):
            out = run(*operands, *before)
            self.result = out[0] if isinstance(out, (list, tuple)) else out
            return out

        return go


def weights_kernel(meta, pattern, interp, out):
    slot = pl.program_id(0) // 2
    level = jnp.where(slot < 2, 1, jnp.where(slot == 2, 0, 2))
    cols = lax.broadcasted_iota(jnp.int32, (1, W), 1) // BLOCK
    named = []
    for k in range(2):
        row = jnp.full((1, W), pattern[level * 8 + k])
        for q in range(1, 4):
            row = jnp.where(cols == q, pattern[level * 8 + q * 2 + k], row)
        named.append(row)
    for p in range(4):
        at = slice(p * BLOCK, p * BLOCK + BLOCK)
        w = interp[0, 0, 0, at, :].astype(F32)
        out[0, at, :] = jnp.where((named[0] == p) | (named[1] == p), w, 0.0).astype(BF)


def weights(call, meta, pattern, interp):
    def pick(t, meta, pattern):
        slot = t // 2
        level = jnp.where(slot < 2, 1, jnp.where(slot == 2, 0, 2))
        bit = meta[level]
        return level, bit ^ jnp.where(slot == 1, 1, 0), bit ^ (t & 1), 0, 0

    return call(
        weights_kernel, "masked_weights", (8,),
        [pl.BlockSpec((1, 1, 1, W, W), pick)],
        pl.BlockSpec((1, W, W), lambda t, *_: (t // 2, t % 2, 0)),
        jax.ShapeDtypeStruct((4, 2 * W, W), BF), prefetch=2, flops=0, nbytes=2 << 20,
    )(meta, pattern, interp)


def first_kernel(shuffle, coeffs, angles, out):
    for a in range(2):
        for i in range(STEP):
            x = jnp.concatenate([coeffs[a, i, : 2 * SB], coeffs[a, i, 2 * SB :]], axis=1)
            y = dot(shuffle[...], x)
            for part in range(2):
                lanes = slice(part * 128, part * 128 + 128)
                for r in range(0, 64, 32):
                    row = [y[k * 64 + r : k * 64 + r + 32, lanes] for k in range(4)]
                    at = part * 64 + r
                    re, im = turn(
                        jnp.concatenate(row[:2], axis=1), jnp.concatenate(row[2:], axis=1), angles[0, a, i, at : at + 32]
                    )
                    out[a, i, at : at + 32, :W] = re
                    out[a, i, at : at + 32, W:] = im


def first(call, shuffle, coeffs, angles, off, n):
    return call(
        first_kernel, "rotate_0", (n // STEP,),
        [
            pl.BlockSpec((W, W), lambda t: (0, 0)),
            pl.BlockSpec((2, STEP, 4 * SB, 128), lambda t: (0, off // STEP + t, 0, 0)),
            pl.BlockSpec((1, 2, STEP, SB, W), lambda t: (0, 0, off // STEP + t, 0, 0)),
        ],
        pl.BlockSpec((2, STEP, SB, 2 * W), lambda t: (0, t, 0, 0)),
        jax.ShapeDtypeStruct((2, n, SB, 2 * W), BF), flops=n * 2e8, nbytes=n * 700e3, limit=FIRST_LIMIT,
    )(shuffle, coeffs, angles)


def sides(own, other):
    return jnp.concatenate(
        [jnp.concatenate([own[:, :W], other[:, :W]], axis=1), jnp.concatenate([own[:, W : 2 * W], other[:, W : 2 * W]], axis=1)], axis=0
    )


def turn_rows(y, angles, store):
    for r in range(0, SB, 32):
        re, im = turn(y[r : r + 32], y[SB + r : SB + r + 32], angles[r : r + 32])
        store(r, re, im)


def second_kernel(meta, own, other, w, angles, ahead, keep, send):
    h = meta[3]
    send[:, :, 2 * W :] = ahead[0, 0]
    for out, a in ((send, 1 - h), (keep, h)):
        for i in range(STEP):
            y = dot(sides(own[a, i], other[a, i]), w[0])

            def store(r, re, im, out=out, i=i):
                out[i, r : r + 32, :W] = re
                out[i, r : r + 32, W : 2 * W] = im

            turn_rows(y, angles.at[0, a, i], store)


def second(call, meta, own, other, w, angles, off, n):
    both = pl.BlockSpec((2, STEP, SB, 2 * W), lambda t, *_: (0, t, 0, 0))
    return call(
        second_kernel, "mix_0_rotate_1", (n // STEP,),
        [
            both,
            both,
            pl.BlockSpec((1, 2 * W, W), lambda t, *_: (2, 0, 0)),
            pl.BlockSpec((1, 2, STEP, SB, W), lambda t, *_: (1, 0, off // STEP + t, 0, 0)),
            pl.BlockSpec((1, 1, STEP, SB, W), lambda t, meta: (2, 1 - meta[3], off // STEP + t, 0, 0)),
        ],
        [
            pl.BlockSpec((STEP, SB, 2 * W), lambda t, *_: (t, 0, 0)),
            pl.BlockSpec((STEP, SB, 3 * W), lambda t, *_: (t, 0, 0)),
        ],
        [jax.ShapeDtypeStruct((n, SB, 2 * W), BF), jax.ShapeDtypeStruct((n, SB, 3 * W), BF)],
        prefetch=1, flops=n * 2e8, nbytes=n * 1e6,
    )(meta, own, other, w, angles, angles)


def third_kernel(meta, own, other, w, angles, out):
    for i in range(STEP):
        x = sides(own[i], other[i])
        for g, angle in ((0, angles.at[0, 0, i]), (1, other.at[i, :, 2 * W :])):
            y = dot(x, w[g])

            def store(r, re, im, g=g, i=i):
                out[g, i, r : r + 32, :W] = re
                out[g, i, r : r + 32, W:] = im

            turn_rows(y, angle, store)


def third(call, meta, own, other, w, angles, off, n):
    return call(
        third_kernel, "mix_1_rotate_2", (n // STEP,),
        [
            pl.BlockSpec((STEP, SB, 2 * W), lambda t, *_: (t, 0, 0)),
            pl.BlockSpec((STEP, SB, 3 * W), lambda t, *_: (t, 0, 0)),
            pl.BlockSpec((2, 2 * W, W), lambda t, *_: (0, 0, 0)),
            pl.BlockSpec((1, 1, STEP, SB, W), lambda t, meta: (2, meta[3], off // STEP + t, 0, 0)),
        ],
        pl.BlockSpec((2, STEP, SB, 2 * W), lambda t, *_: (0, t, 0, 0)),
        jax.ShapeDtypeStruct((2, n, SB, 2 * W), BF), prefetch=1, flops=n * 2e8, nbytes=n * 700e3,
    )(meta, own, other, w, angles)


def back_kernel(own, other, w, out):
    for i in range(STEP):
        y = dot(sides(own[0, i], other[0, i]), w[0])
        out[i, :, :W] = y[:SB].astype(BF)
        out[i, :, W:] = y[SB:].astype(BF)


def back(call, own, other, w, n):
    return call(
        back_kernel, "mix_2_other", (n // STEP,),
        [
            pl.BlockSpec((1, STEP, SB, 2 * W), lambda t: (1, t, 0, 0)),
            pl.BlockSpec((1, STEP, SB, 2 * W), lambda t: (0, t, 0, 0)),
            pl.BlockSpec((1, 2 * W, W), lambda t: (3, 0, 0)),
        ],
        pl.BlockSpec((STEP, SB, 2 * W), lambda t: (t, 0, 0)),
        jax.ShapeDtypeStruct((n, SB, 2 * W), BF), flops=n * 1e8, nbytes=n * 400e3,
    )(own, other, w)


def split_kernel(own, other, w, came, out):
    for i in range(STEP):
        y = dot(sides(own[0, i], other[0, i]), w[0]).astype(BF)
        for q in range(8):
            out[q, 0, i, :, :W] = y[q * 16 : q * 16 + 16]
            out[q, 0, i, :, W:] = y[SB + q * 16 : SB + q * 16 + 16]
            out[q, 1, i] = came[i, q * 16 : q * 16 + 16]


def split(call, own, other, w, came, n):
    return call(
        split_kernel, "mix_2_own_split", (n // STEP,),
        [
            pl.BlockSpec((1, STEP, SB, 2 * W), lambda t: (0, t, 0, 0)),
            pl.BlockSpec((1, STEP, SB, 2 * W), lambda t: (1, t, 0, 0)),
            pl.BlockSpec((1, 2 * W, W), lambda t: (3, 0, 0)),
            pl.BlockSpec((STEP, SB, 2 * W), lambda t: (t, 0, 0)),
        ],
        pl.BlockSpec((8, 2, STEP, 16, 2 * W), lambda t: (0, 0, t, 0, 0)),
        jax.ShapeDtypeStruct((8, 2, n, 16, 2 * W), BF), flops=n * 1e8, nbytes=n * 800e3,
    )(own, other, w, came)


def gather_kernel(shuffle, pieces, out):
    y = dot(shuffle[...], pieces[...].reshape(W, 2 * W)).astype(BF)
    for j in range(16):
        out[j] = y[j * 16 : j * 16 + 16]


def gather(call, shuffle, pieces, n):
    return call(
        gather_kernel, "gather_frequencies", (n,),
        [pl.BlockSpec((W, W), lambda t: (0, 0)), pl.BlockSpec((8 // n, 2, n, 16, 2 * W), lambda t: (t, 0, 0, 0, 0))],
        pl.BlockSpec((16, 16, 2 * W), lambda t: (0, t, 0)),
        jax.ShapeDtypeStruct((16, 16 * n, 2 * W), BF), flops=n * 1e8, nbytes=n * 500e3,
    )(shuffle, pieces)


def target_kernel(chunks, t_map, *refs):
    parts, out = refs[:chunks], refs[chunks]
    for j in range(2):
        y = dot(t_map[...], jnp.concatenate([p[j] for p in parts], axis=0))
        for c in range(2):
            for half in range(2):
                at = c * W + half * 128
                out[:, j * 4 + half * 2 + c, :] = y[:, at : at + 128]


def target(call, t_map, parts):
    return call(
        functools.partial(target_kernel, len(parts)), "target_map", (8,),
        [pl.BlockSpec((W, W), lambda t: (0, 0))]
        + [pl.BlockSpec((2, p.shape[1], 2 * W), lambda t: (t, 0, 0)) for p in parts],
        pl.BlockSpec((W, 8, 128), lambda t: (0, t, 0)),
        jax.ShapeDtypeStruct((W, 64, 128), F32), flops=1e9, nbytes=12 << 20,
    )(t_map, *parts)


def swap(value, axis, mask):
    return lax.ppermute(value, axis, [(i, i ^ mask) for i in range(lax.axis_size(axis))])


def shuffles():
    first_rows = np.zeros((W, W), np.float32)
    last_rows = np.zeros((W, W), np.float32)
    for j in range(64):
        for half in range(2):
            for c in range(2):
                first_rows[(c * 2 + half) * 64 + j, j * 4 + half * 2 + c] = 1
    for j in range(16):
        for f in range(16):
            last_rows[j * 16 + f, f * 16 + j] = 1
    return jnp.asarray(first_rows, BF), jnp.asarray(last_rows, BF)


def on_device(coeffs, angles, interp, pattern, target_map):
    src = lax.axis_index("src")
    bits = [src >> k & 1 for k in range(LEVELS)]
    h = bits[1] ^ bits[2]
    meta = jnp.stack([*bits, h]).astype(jnp.int32)
    spread, close = shuffles()
    coeffs = coeffs.reshape(2, 16, SB, 2, 2, 128).transpose(0, 1, 2, 4, 3, 5).reshape(2, 16, 4 * SB, 128)
    angles = angles.reshape(LEVELS, 2, 16, SB, W)

    offs = np.cumsum((0,) + CHUNKS)[:-1].tolist()
    order = np.concatenate(
        [
            np.asarray([m << 5 | half << 4 | off + i for m in range(8) for half in range(2) for i in range(n)])
            for off, n in zip(offs, CHUNKS)
        ]
    )
    chosen = jnp.asarray(order, jnp.int32) ^ (h << 4)
    hot = (jnp.arange(W, dtype=jnp.int32)[:, None] == chosen[None, :]).astype(BF)
    t_map = jnp.dot(target_map, hot, preferred_element_type=F32).astype(BF)

    call = Order()
    state, done = {}, {}

    def step(kind, c):
        w = state.get("w")
        if kind == "W":
            state["w"] = weights(call, meta, pattern.reshape(-1), interp)
            return
        off, n = offs[c], CHUNKS[c]
        if kind == "F":
            turned = first(call, spread, coeffs, angles, off, n)
            state["F", c] = turned, swap(turned, "src", 1)
        if kind == "S":
            keep, send = second(call, meta, *state["F", c], w, angles, off, n)
            state["S", c] = keep, swap(send, "src", 2)
        if kind == "T":
            turned = third(call, meta, *state["S", c], w, angles, off, n)
            state["T", c] = turned, swap(turned, "src", 6)
        if kind == "B":
            state["B", c] = swap(back(call, *state["T", c], w, n), "src", 2)
        if kind == "X":
            pieces = split(call, *state["T", c], w, state["B", c], n)
            pieces = lax.all_to_all(pieces.reshape(-1, 2 * W), "frq", 0, 0, tiled=True)
            state["X", c] = pieces.reshape(8, 2, n, 16, 2 * W)
        if kind == "G":
            state["G", c] = gather(call, close, state["X", c], n)

    for name in STEPS:
        call.last = [done[other] for other in AFTER.get(name, ())]
        step(name[0], int(name[1:]))
        done[name] = call.result
    call.last = []
    parts = [state["G", c] for c in range(len(CHUNKS))]
    out = target(call, t_map, parts)
    return out.reshape(W, 16, 2, 2, 128).transpose(0, 1, 3, 2, 4).reshape(W, 16, 2, W)


def solution(mesh):
    return jax.shard_map(
        on_device,
        mesh=mesh,
        in_specs=(P("frq", "src", None, None), P(None, "frq", "src", None), P(), P(), P()),
        out_specs=P(None, ("src", "frq"), None, None),
        check_vma=False,
    )
```

```python
import functools

import jax
import jax.numpy as jnp
import numpy as np
from jax import lax
from jax.experimental import pallas as pl
from jax.experimental.pallas import tpu as pltpu
from jax.sharding import PartitionSpec as P

BLOCK = 64
LEVELS = 3
CHUNKS = (4, 4, 4, 4)
STEPS = (
    "F0", "F1", "W0", "S0", "S1", "T0", "S2", "T1", "S3", "B0", "T2", "X0",
    "B1", "G0", "T3", "X1", "B2", "G1", "X2", "B3", "G2", "X3", "G3",
)
AFTER = {"F1": ("F0",), "W0": ("F1",), "S0": ("W0",), "S1": ("S0",), "T0": ("S1",), "S2": ("T0",), "T1": ("S2",), "S3": ("T1",), "B0": ("S3",), "T2": ("B0",), "X0": ("T2",), "B1": ("X0",), "G0": ("B1",), "T3": ("G0",), "X1": ("T3",), "B2": ("X1",), "G1": ("B2",), "X2": ("G1",), "B3": ("X2",), "G2": ("B3",), "X3": ("G2",), "G3": ("X3",)}
STEP = 2
FIRST_LIMIT = 60
FIRST = ((0,), (1, 2, 3))
LIMIT = 40
COST = 20.0
SB = 128
W = 256
BF = jnp.bfloat16
F32 = jnp.float32

_x = np.cos((np.arange(400) + 0.5) * np.pi / 400) * 3.1410
_u = (_x * _x) / 10.0
COS = np.linalg.lstsq(np.stack([_u**k for k in range(6)], 1), np.cos(_x), rcond=None)[0]
SIN = np.linalg.lstsq(np.stack([_x * _u**k for k in range(5)], 1), np.sin(_x), rcond=None)[0]
COS = [float(c / 10.0**k) for k, c in enumerate(COS)]
SIN = [float(c / 10.0**k) for k, c in enumerate(SIN)]


def cos_sin(x):
    u = x * x
    c = COS[5] * u + COS[4]
    for k in (3, 2, 1, 0):
        c = c * u + COS[k]
    s = SIN[4] * u + SIN[3]
    for k in (2, 1, 0):
        s = s * u + SIN[k]
    return c, s * x


def turn(re, im, angle):
    c, s = cos_sin(angle.astype(F32))
    return (re * c - im * s).astype(BF), (re * s + im * c).astype(BF)


def dot(a, b):
    return jnp.dot(a, b, preferred_element_type=F32)


class Order:
    def __init__(self):
        self.last = []

    def __call__(self, kernel, name, grid, in_specs, out_specs, out_shape, prefetch=0, scratch=(), flops=0, nbytes=0, limit=None):
        at = prefetch + len(in_specs)

        def body(*refs):
            kernel(*refs[:at], *refs[at + len(before) :])

        before = list(self.last)
        run = pl.pallas_call(
            body,
            out_shape=out_shape,
            grid_spec=pltpu.PrefetchScalarGridSpec(
                num_scalar_prefetch=prefetch,
                grid=grid,
                in_specs=list(in_specs) + [pl.BlockSpec(memory_space=pl.ANY)] * len(before),
                out_specs=out_specs,
                scratch_shapes=list(scratch),
            ),
            compiler_params=pltpu.CompilerParams(vmem_limit_bytes=(limit or LIMIT) << 20),
            cost_estimate=pl.CostEstimate(flops=int(flops * COST), bytes_accessed=int(nbytes * COST), transcendentals=0),
            name=name,
        )

        def go(*operands):
            out = run(*operands, *before)
            self.result = out[0] if isinstance(out, (list, tuple)) else out
            return out

        return go


def weights_kernel(meta, pattern, interp, out):
    slot = pl.program_id(0) // 2
    level = jnp.where(slot < 2, 1, jnp.where(slot == 2, 0, 2))
    cols = lax.broadcasted_iota(jnp.int32, (1, W), 1) // BLOCK
    named = []
    for k in range(2):
        row = jnp.full((1, W), pattern[level * 8 + k])
        for q in range(1, 4):
            row = jnp.where(cols == q, pattern[level * 8 + q * 2 + k], row)
        named.append(row)
    for p in range(4):
        at = slice(p * BLOCK, p * BLOCK + BLOCK)
        w = interp[0, 0, 0, at, :].astype(F32)
        out[0, at, :] = jnp.where((named[0] == p) | (named[1] == p), w, 0.0).astype(BF)


def weights(call, meta, pattern, interp):
    def pick(t, meta, pattern):
        slot = t // 2
        level = jnp.where(slot < 2, 1, jnp.where(slot == 2, 0, 2))
        bit = meta[level]
        return level, bit ^ jnp.where(slot == 1, 1, 0), bit ^ (t & 1), 0, 0

    return call(
        weights_kernel, "masked_weights", (8,),
        [pl.BlockSpec((1, 1, 1, W, W), pick)],
        pl.BlockSpec((1, W, W), lambda t, *_: (t // 2, t % 2, 0)),
        jax.ShapeDtypeStruct((4, 2 * W, W), BF), prefetch=2, flops=0, nbytes=2 << 20,
    )(meta, pattern, interp)


def first_kernel(ahead, meta, shuffle, coeffs, angles, *refs):
    out = refs[-2] if ahead else refs[-1]
    if ahead:
        refs[-1][...] = refs[0][0, 0]
    for a in range(2):
        for i in range(STEP):
            x = jnp.concatenate([coeffs[a, i, : 2 * SB], coeffs[a, i, 2 * SB :]], axis=1)
            y = dot(shuffle[...], x)
            for part in range(2):
                lanes = slice(part * 128, part * 128 + 128)
                for r in range(0, 64, 32):
                    row = [y[k * 64 + r : k * 64 + r + 32, lanes] for k in range(4)]
                    at = part * 64 + r
                    re, im = turn(
                        jnp.concatenate(row[:2], axis=1), jnp.concatenate(row[2:], axis=1), angles[0, a, i, at : at + 32]
                    )
                    out[a, i, at : at + 32, :W] = re
                    out[a, i, at : at + 32, W:] = im


def first(call, meta, shuffle, coeffs, angles, off, n, ahead):
    steps = n // STEP
    out_specs = [pl.BlockSpec((2, STEP, SB, 2 * W), lambda t, *_: (0, t, 0, 0))]
    shapes = [jax.ShapeDtypeStruct((2, n, SB, 2 * W), BF)]
    in_specs = [
        pl.BlockSpec((W, W), lambda t, *_: (0, 0)),
        pl.BlockSpec((2, STEP, 4 * SB, 128), lambda t, *_: (0, off // STEP + t, 0, 0)),
        pl.BlockSpec((1, 2, STEP, SB, W), lambda t, *_: (0, 0, off // STEP + t, 0, 0)),
    ]
    if ahead:
        in_specs.append(pl.BlockSpec((1, 1, 16 // steps, SB, W), lambda t, meta: (2, 1 - meta[3], t, 0, 0)))
        out_specs.append(pl.BlockSpec((16 // steps, SB, W), lambda t, *_: (t, 0, 0)))
        shapes.append(jax.ShapeDtypeStruct((16, SB, W), BF))
    return call(
        functools.partial(first_kernel, ahead), "rotate_0", (steps,), in_specs, out_specs, shapes,
        prefetch=1, flops=n * 2e8, nbytes=n * 700e3, limit=FIRST_LIMIT,
    )(meta, shuffle, coeffs, angles, *([angles] if ahead else []))


def sides(own, other):
    return jnp.concatenate(
        [jnp.concatenate([own[:, :W], other[:, :W]], axis=1), jnp.concatenate([own[:, W : 2 * W], other[:, W : 2 * W]], axis=1)], axis=0
    )


def turn_rows(y, angles, store):
    for r in range(0, SB, 32):
        re, im = turn(y[r : r + 32], y[SB + r : SB + r + 32], angles[r : r + 32])
        store(r, re, im)


def second_kernel(meta, own, other, w, angles, keep, send):
    h = meta[3]
    for out, a in ((send, 1 - h), (keep, h)):
        for i in range(STEP):
            y = dot(sides(own[a, i], other[a, i]), w[0])

            def store(r, re, im, out=out, i=i):
                out[i, r : r + 32, :W] = re
                out[i, r : r + 32, W:] = im

            turn_rows(y, angles.at[0, a, i], store)


def second(call, meta, own, other, w, angles, off, skip, n):
    both = pl.BlockSpec((2, STEP, SB, 2 * W), lambda t, *_: (0, (off - skip) // STEP + t, 0, 0))
    one = pl.BlockSpec((STEP, SB, 2 * W), lambda t, *_: (t, 0, 0))
    return call(
        second_kernel, "mix_0_rotate_1", (n // STEP,),
        [
            both,
            both,
            pl.BlockSpec((1, 2 * W, W), lambda t, *_: (2, 0, 0)),
            pl.BlockSpec((1, 2, STEP, SB, W), lambda t, *_: (1, 0, off // STEP + t, 0, 0)),
        ],
        [one, one],
        [jax.ShapeDtypeStruct((n, SB, 2 * W), BF)] * 2,
        prefetch=1, flops=n * 2e8, nbytes=n * 1e6,
    )(meta, own, other, w, angles)


def third_kernel(meta, own, other, w, angles, angles_other, out):
    for i in range(STEP):
        x = sides(own[i], other[i])
        for g, angle in ((0, angles.at[0, 0, i]), (1, angles_other.at[i])):
            y = dot(x, w[g])

            def store(r, re, im, g=g, i=i):
                out[g, i, r : r + 32, :W] = re
                out[g, i, r : r + 32, W:] = im

            turn_rows(y, angle, store)


def third(call, meta, own, other, w, angles, angles_other, off, n):
    one = pl.BlockSpec((STEP, SB, 2 * W), lambda t, *_: (t, 0, 0))
    return call(
        third_kernel, "mix_1_rotate_2", (n // STEP,),
        [
            one,
            one,
            pl.BlockSpec((2, 2 * W, W), lambda t, *_: (0, 0, 0)),
            pl.BlockSpec((1, 1, STEP, SB, W), lambda t, meta: (2, meta[3], off // STEP + t, 0, 0)),
            pl.BlockSpec((STEP, SB, W), lambda t, *_: (off // STEP + t, 0, 0)),
        ],
        pl.BlockSpec((2, STEP, SB, 2 * W), lambda t, *_: (0, t, 0, 0)),
        jax.ShapeDtypeStruct((2, n, SB, 2 * W), BF), prefetch=1, flops=n * 2e8, nbytes=n * 700e3,
    )(meta, own, other, w, angles, angles_other)


def back_kernel(own, other, w, out):
    for i in range(STEP):
        y = dot(sides(own[0, i], other[0, i]), w[0])
        out[i, :, :W] = y[:SB].astype(BF)
        out[i, :, W:] = y[SB:].astype(BF)


def back(call, own, other, w, n):
    return call(
        back_kernel, "mix_2_other", (n // STEP,),
        [
            pl.BlockSpec((1, STEP, SB, 2 * W), lambda t: (1, t, 0, 0)),
            pl.BlockSpec((1, STEP, SB, 2 * W), lambda t: (0, t, 0, 0)),
            pl.BlockSpec((1, 2 * W, W), lambda t: (3, 0, 0)),
        ],
        pl.BlockSpec((STEP, SB, 2 * W), lambda t: (t, 0, 0)),
        jax.ShapeDtypeStruct((n, SB, 2 * W), BF), flops=n * 1e8, nbytes=n * 400e3,
    )(own, other, w)


def split_kernel(own, other, w, came, out):
    for i in range(STEP):
        y = dot(sides(own[0, i], other[0, i]), w[0]).astype(BF)
        for q in range(8):
            out[q, 0, i, :, :W] = y[q * 16 : q * 16 + 16]
            out[q, 0, i, :, W:] = y[SB + q * 16 : SB + q * 16 + 16]
            out[q, 1, i] = came[i, q * 16 : q * 16 + 16]


def split(call, own, other, w, came, n):
    return call(
        split_kernel, "mix_2_own_split", (n // STEP,),
        [
            pl.BlockSpec((1, STEP, SB, 2 * W), lambda t: (0, t, 0, 0)),
            pl.BlockSpec((1, STEP, SB, 2 * W), lambda t: (1, t, 0, 0)),
            pl.BlockSpec((1, 2 * W, W), lambda t: (3, 0, 0)),
            pl.BlockSpec((STEP, SB, 2 * W), lambda t: (t, 0, 0)),
        ],
        pl.BlockSpec((8, 2, STEP, 16, 2 * W), lambda t: (0, 0, t, 0, 0)),
        jax.ShapeDtypeStruct((8, 2, n, 16, 2 * W), BF), flops=n * 1e8, nbytes=n * 800e3,
    )(own, other, w, came)


def gather_kernel(shuffle, pieces, out):
    y = dot(shuffle[...], pieces[...].reshape(W, 2 * W)).astype(BF)
    for j in range(16):
        out[j] = y[j * 16 : j * 16 + 16]


def gather(call, shuffle, pieces, n):
    return call(
        gather_kernel, "gather_frequencies", (n,),
        [pl.BlockSpec((W, W), lambda t: (0, 0)), pl.BlockSpec((8 // n, 2, n, 16, 2 * W), lambda t: (t, 0, 0, 0, 0))],
        pl.BlockSpec((16, 16, 2 * W), lambda t: (0, t, 0)),
        jax.ShapeDtypeStruct((16, 16 * n, 2 * W), BF), flops=n * 1e8, nbytes=n * 500e3,
    )(shuffle, pieces)


def target_kernel(chunks, t_map, *refs):
    parts, out = refs[:chunks], refs[chunks]
    for j in range(2):
        y = dot(t_map[...], jnp.concatenate([p[j] for p in parts], axis=0))
        for c in range(2):
            for half in range(2):
                at = c * W + half * 128
                out[:, j * 4 + half * 2 + c, :] = y[:, at : at + 128]


def target(call, t_map, parts):
    return call(
        functools.partial(target_kernel, len(parts)), "target_map", (8,),
        [pl.BlockSpec((W, W), lambda t: (0, 0))]
        + [pl.BlockSpec((2, p.shape[1], 2 * W), lambda t: (t, 0, 0)) for p in parts],
        pl.BlockSpec((W, 8, 128), lambda t: (0, t, 0)),
        jax.ShapeDtypeStruct((W, 64, 128), F32), flops=1e9, nbytes=12 << 20,
    )(t_map, *parts)


def swap(value, axis, mask):
    return lax.ppermute(value, axis, [(i, i ^ mask) for i in range(lax.axis_size(axis))])


def shuffles():
    first_rows = np.zeros((W, W), np.float32)
    last_rows = np.zeros((W, W), np.float32)
    for j in range(64):
        for half in range(2):
            for c in range(2):
                first_rows[(c * 2 + half) * 64 + j, j * 4 + half * 2 + c] = 1
    for j in range(16):
        for f in range(16):
            last_rows[j * 16 + f, f * 16 + j] = 1
    return jnp.asarray(first_rows, BF), jnp.asarray(last_rows, BF)


def on_device(coeffs, angles, interp, pattern, target_map):
    src = lax.axis_index("src")
    bits = [src >> k & 1 for k in range(LEVELS)]
    h = bits[1] ^ bits[2]
    meta = jnp.stack([*bits, h]).astype(jnp.int32)
    spread, close = shuffles()
    coeffs = coeffs.reshape(2, 16, SB, 2, 2, 128).transpose(0, 1, 2, 4, 3, 5).reshape(2, 16, 4 * SB, 128)
    angles = angles.reshape(LEVELS, 2, 16, SB, W)

    offs = np.cumsum((0,) + CHUNKS)[:-1].tolist()
    order = np.concatenate(
        [
            np.asarray([m << 5 | half << 4 | off + i for m in range(8) for half in range(2) for i in range(n)])
            for off, n in zip(offs, CHUNKS)
        ]
    )
    chosen = jnp.asarray(order, jnp.int32) ^ (h << 4)
    hot = (jnp.arange(W, dtype=jnp.int32)[:, None] == chosen[None, :]).astype(BF)
    t_map = jnp.dot(target_map, hot, preferred_element_type=F32).astype(BF)

    call = Order()
    state, done = {}, {}

    def step(kind, c):
        w = state.get("w")
        if kind == "W":
            state["w"] = weights(call, meta, pattern.reshape(-1), interp)
            return
        off, n = (offs[c], CHUNKS[c]) if kind != "F" else (0, 0)
        if kind == "F":
            group = FIRST[c]
            skip, ahead = offs[group[0]], c == 0
            turned = first(call, meta, spread, coeffs, angles, skip, sum(CHUNKS[k] for k in group), ahead)
            if ahead:
                state["A"] = swap(turned[1], "src", 2)
            other = swap(turned[0], "src", 1)
            for k in group:
                state["F", k] = turned[0], other, skip
        if kind == "S":
            own, other, skip = state["F", c]
            keep, send = second(call, meta, own, other, w, angles, off, skip, n)
            state["S", c] = keep, swap(send, "src", 2)
        if kind == "T":
            turned = third(call, meta, *state["S", c], w, angles, state["A"], off, n)
            state["T", c] = turned, swap(turned, "src", 6)
        if kind == "B":
            state["B", c] = swap(back(call, *state["T", c], w, n), "src", 2)
        if kind == "X":
            pieces = split(call, *state["T", c], w, state["B", c], n)
            pieces = lax.all_to_all(pieces.reshape(-1, 2 * W), "frq", 0, 0, tiled=True)
            state["X", c] = pieces.reshape(8, 2, n, 16, 2 * W)
        if kind == "G":
            state["G", c] = gather(call, close, state["X", c], n)

    for name in STEPS:
        call.last = [done[other] for other in AFTER.get(name, ())]
        step(name[0], int(name[1:]))
        done[name] = call.result
    call.last = []
    parts = [state["G", c] for c in range(len(CHUNKS))]
    out = target(call, t_map, parts)
    return out.reshape(W, 16, 2, 2, 128).transpose(0, 1, 3, 2, 4).reshape(W, 16, 2, W)


def solution(mesh):
    return jax.shard_map(
        on_device,
        mesh=mesh,
        in_specs=(P("frq", "src", None, None), P(None, "frq", "src", None), P(), P(), P()),
        out_specs=P(None, ("src", "frq"), None, None),
        check_vma=False,
    )
```

```python
import functools

import jax
import jax.numpy as jnp
import numpy as np
from jax import lax
from jax.experimental import pallas as pl
from jax.experimental.pallas import tpu as pltpu
from jax.sharding import PartitionSpec as P

BLOCK = 64
LEVELS = 3
CHUNKS = (4, 4, 4, 4)
STEPS = (
    "F0", "F1", "W0", "S0", "S1", "T0", "S2", "T1", "S3", "B0", "T2", "X0",
    "B1", "G0", "T3", "X1", "B2", "G1", "X2", "B3", "G2", "X3", "G3",
)
AFTER = {"F1": ("F0",), "W0": ("F1",), "S0": ("W0",), "S1": ("S0",), "T0": ("S1",), "S2": ("T0",), "T1": ("S2",), "S3": ("T1",), "B0": ("S3",), "T2": ("B0",), "X0": ("T2",), "B1": ("X0",), "G0": ("B1",), "T3": ("G0",), "X1": ("T3",), "B2": ("X1",), "G1": ("B2",), "X2": ("G1",), "B3": ("X2",), "G2": ("B3",), "X3": ("G2",), "G3": ("X3",)}
LIGHT = ("G0", "T3", "X1", "B2", "G1", "X2", "B3", "G2", "X3", "G3")
STEP = 2
FIRST_LIMIT = 60
FIRST = ((0,), (1, 2, 3))
LIMIT = 40
COST = 20.0
SB = 128
W = 256
BF = jnp.bfloat16
F32 = jnp.float32

_x = np.cos((np.arange(400) + 0.5) * np.pi / 400) * 3.1410
_u = (_x * _x) / 10.0
COS = np.linalg.lstsq(np.stack([_u**k for k in range(6)], 1), np.cos(_x), rcond=None)[0]
SIN = np.linalg.lstsq(np.stack([_x * _u**k for k in range(5)], 1), np.sin(_x), rcond=None)[0]
COS = [float(c / 10.0**k) for k, c in enumerate(COS)]
SIN = [float(c / 10.0**k) for k, c in enumerate(SIN)]


def cos_sin(x):
    u = x * x
    c = COS[5] * u + COS[4]
    for k in (3, 2, 1, 0):
        c = c * u + COS[k]
    s = SIN[4] * u + SIN[3]
    for k in (2, 1, 0):
        s = s * u + SIN[k]
    return c, s * x


def turn(re, im, angle):
    c, s = cos_sin(angle.astype(F32))
    return (re * c - im * s).astype(BF), (re * s + im * c).astype(BF)


def dot(a, b):
    return jnp.dot(a, b, preferred_element_type=F32)


class Order:
    def __init__(self):
        self.last = []
        self.scale = COST

    def __call__(self, kernel, name, grid, in_specs, out_specs, out_shape, prefetch=0, scratch=(), flops=0, nbytes=0, limit=None):
        at = prefetch + len(in_specs)

        def body(*refs):
            kernel(*refs[:at], *refs[at + len(before) :])

        before, scale = list(self.last), self.scale
        run = pl.pallas_call(
            body,
            out_shape=out_shape,
            grid_spec=pltpu.PrefetchScalarGridSpec(
                num_scalar_prefetch=prefetch,
                grid=grid,
                in_specs=list(in_specs) + [pl.BlockSpec(memory_space=pl.ANY)] * len(before),
                out_specs=out_specs,
                scratch_shapes=list(scratch),
            ),
            compiler_params=pltpu.CompilerParams(vmem_limit_bytes=(limit or LIMIT) << 20),
            cost_estimate=pl.CostEstimate(flops=int(flops * scale), bytes_accessed=int(nbytes * scale), transcendentals=0),
            name=name,
        )

        def go(*operands):
            out = run(*operands, *before)
            self.result = out[0] if isinstance(out, (list, tuple)) else out
            return out

        return go


def weights_kernel(meta, pattern, interp, out):
    slot = pl.program_id(0) // 2
    level = jnp.where(slot < 2, 1, jnp.where(slot == 2, 0, 2))
    cols = lax.broadcasted_iota(jnp.int32, (1, W), 1) // BLOCK
    named = []
    for k in range(2):
        row = jnp.full((1, W), pattern[level * 8 + k])
        for q in range(1, 4):
            row = jnp.where(cols == q, pattern[level * 8 + q * 2 + k], row)
        named.append(row)
    for p in range(4):
        at = slice(p * BLOCK, p * BLOCK + BLOCK)
        w = interp[0, 0, 0, at, :].astype(F32)
        out[0, at, :] = jnp.where((named[0] == p) | (named[1] == p), w, 0.0).astype(BF)


def weights(call, meta, pattern, interp):
    def pick(t, meta, pattern):
        slot = t // 2
        level = jnp.where(slot < 2, 1, jnp.where(slot == 2, 0, 2))
        bit = meta[level]
        return level, bit ^ jnp.where(slot == 1, 1, 0), bit ^ (t & 1), 0, 0

    return call(
        weights_kernel, "masked_weights", (8,),
        [pl.BlockSpec((1, 1, 1, W, W), pick)],
        pl.BlockSpec((1, W, W), lambda t, *_: (t // 2, t % 2, 0)),
        jax.ShapeDtypeStruct((4, 2 * W, W), BF), prefetch=2, flops=0, nbytes=2 << 20,
    )(meta, pattern, interp)


def first_kernel(ahead, meta, shuffle, coeffs, angles, *refs):
    out = refs[-2] if ahead else refs[-1]
    if ahead:
        refs[-1][...] = refs[0][0, 0]
    for a in range(2):
        for i in range(STEP):
            x = jnp.concatenate([coeffs[a, i, : 2 * SB], coeffs[a, i, 2 * SB :]], axis=1)
            y = dot(shuffle[...], x)
            for part in range(2):
                lanes = slice(part * 128, part * 128 + 128)
                for r in range(0, 64, 32):
                    row = [y[k * 64 + r : k * 64 + r + 32, lanes] for k in range(4)]
                    at = part * 64 + r
                    re, im = turn(
                        jnp.concatenate(row[:2], axis=1), jnp.concatenate(row[2:], axis=1), angles[0, a, i, at : at + 32]
                    )
                    out[a, i, at : at + 32, :W] = re
                    out[a, i, at : at + 32, W:] = im


def first(call, meta, shuffle, coeffs, angles, off, n, ahead):
    steps = n // STEP
    out_specs = [pl.BlockSpec((2, STEP, SB, 2 * W), lambda t, *_: (0, t, 0, 0))]
    shapes = [jax.ShapeDtypeStruct((2, n, SB, 2 * W), BF)]
    in_specs = [
        pl.BlockSpec((W, W), lambda t, *_: (0, 0)),
        pl.BlockSpec((2, STEP, 4 * SB, 128), lambda t, *_: (0, off // STEP + t, 0, 0)),
        pl.BlockSpec((1, 2, STEP, SB, W), lambda t, *_: (0, 0, off // STEP + t, 0, 0)),
    ]
    if ahead:
        in_specs.append(pl.BlockSpec((1, 1, 16 // steps, SB, W), lambda t, meta: (2, 1 - meta[3], t, 0, 0)))
        out_specs.append(pl.BlockSpec((16 // steps, SB, W), lambda t, *_: (t, 0, 0)))
        shapes.append(jax.ShapeDtypeStruct((16, SB, W), BF))
    return call(
        functools.partial(first_kernel, ahead), "rotate_0", (steps,), in_specs, out_specs, shapes,
        prefetch=1, flops=n * 2e8, nbytes=n * 700e3, limit=FIRST_LIMIT,
    )(meta, shuffle, coeffs, angles, *([angles] if ahead else []))


def sides(own, other):
    return jnp.concatenate(
        [jnp.concatenate([own[:, :W], other[:, :W]], axis=1), jnp.concatenate([own[:, W : 2 * W], other[:, W : 2 * W]], axis=1)], axis=0
    )


def turn_rows(y, angles, store):
    for r in range(0, SB, 32):
        re, im = turn(y[r : r + 32], y[SB + r : SB + r + 32], angles[r : r + 32])
        store(r, re, im)


def second_kernel(meta, own, other, w, angles, keep, send):
    h = meta[3]
    for out, a in ((send, 1 - h), (keep, h)):
        for i in range(STEP):
            y = dot(sides(own[a, i], other[a, i]), w[0])

            def store(r, re, im, out=out, i=i):
                out[i, r : r + 32, :W] = re
                out[i, r : r + 32, W:] = im

            turn_rows(y, angles.at[0, a, i], store)


def second(call, meta, own, other, w, angles, off, skip, n):
    both = pl.BlockSpec((2, STEP, SB, 2 * W), lambda t, *_: (0, (off - skip) // STEP + t, 0, 0))
    one = pl.BlockSpec((STEP, SB, 2 * W), lambda t, *_: (t, 0, 0))
    return call(
        second_kernel, "mix_0_rotate_1", (n // STEP,),
        [
            both,
            both,
            pl.BlockSpec((1, 2 * W, W), lambda t, *_: (2, 0, 0)),
            pl.BlockSpec((1, 2, STEP, SB, W), lambda t, *_: (1, 0, off // STEP + t, 0, 0)),
        ],
        [one, one],
        [jax.ShapeDtypeStruct((n, SB, 2 * W), BF)] * 2,
        prefetch=1, flops=n * 2e8, nbytes=n * 1e6,
    )(meta, own, other, w, angles)


def third_kernel(meta, own, other, w, angles, angles_other, out):
    for i in range(STEP):
        x = sides(own[i], other[i])
        for g, angle in ((0, angles.at[0, 0, i]), (1, angles_other.at[i])):
            y = dot(x, w[g])

            def store(r, re, im, g=g, i=i):
                out[g, i, r : r + 32, :W] = re
                out[g, i, r : r + 32, W:] = im

            turn_rows(y, angle, store)


def third(call, meta, own, other, w, angles, angles_other, off, n):
    one = pl.BlockSpec((STEP, SB, 2 * W), lambda t, *_: (t, 0, 0))
    return call(
        third_kernel, "mix_1_rotate_2", (n // STEP,),
        [
            one,
            one,
            pl.BlockSpec((2, 2 * W, W), lambda t, *_: (0, 0, 0)),
            pl.BlockSpec((1, 1, STEP, SB, W), lambda t, meta: (2, meta[3], off // STEP + t, 0, 0)),
            pl.BlockSpec((STEP, SB, W), lambda t, *_: (off // STEP + t, 0, 0)),
        ],
        pl.BlockSpec((2, STEP, SB, 2 * W), lambda t, *_: (0, t, 0, 0)),
        jax.ShapeDtypeStruct((2, n, SB, 2 * W), BF), prefetch=1, flops=n * 2e8, nbytes=n * 700e3,
    )(meta, own, other, w, angles, angles_other)


def back_kernel(own, other, w, out):
    for i in range(STEP):
        y = dot(sides(own[0, i], other[0, i]), w[0])
        out[i, :, :W] = y[:SB].astype(BF)
        out[i, :, W:] = y[SB:].astype(BF)


def back(call, own, other, w, n):
    return call(
        back_kernel, "mix_2_other", (n // STEP,),
        [
            pl.BlockSpec((1, STEP, SB, 2 * W), lambda t: (1, t, 0, 0)),
            pl.BlockSpec((1, STEP, SB, 2 * W), lambda t: (0, t, 0, 0)),
            pl.BlockSpec((1, 2 * W, W), lambda t: (3, 0, 0)),
        ],
        pl.BlockSpec((STEP, SB, 2 * W), lambda t: (t, 0, 0)),
        jax.ShapeDtypeStruct((n, SB, 2 * W), BF), flops=n * 1e8, nbytes=n * 400e3,
    )(own, other, w)


def split_kernel(own, other, w, came, out):
    for i in range(STEP):
        y = dot(sides(own[0, i], other[0, i]), w[0]).astype(BF)
        for q in range(8):
            out[q, 0, i, :, :W] = y[q * 16 : q * 16 + 16]
            out[q, 0, i, :, W:] = y[SB + q * 16 : SB + q * 16 + 16]
            out[q, 1, i] = came[i, q * 16 : q * 16 + 16]


def split(call, own, other, w, came, n):
    return call(
        split_kernel, "mix_2_own_split", (n // STEP,),
        [
            pl.BlockSpec((1, STEP, SB, 2 * W), lambda t: (0, t, 0, 0)),
            pl.BlockSpec((1, STEP, SB, 2 * W), lambda t: (1, t, 0, 0)),
            pl.BlockSpec((1, 2 * W, W), lambda t: (3, 0, 0)),
            pl.BlockSpec((STEP, SB, 2 * W), lambda t: (t, 0, 0)),
        ],
        pl.BlockSpec((8, 2, STEP, 16, 2 * W), lambda t: (0, 0, t, 0, 0)),
        jax.ShapeDtypeStruct((8, 2, n, 16, 2 * W), BF), flops=n * 1e8, nbytes=n * 800e3,
    )(own, other, w, came)


def gather_kernel(shuffle, pieces, out):
    y = dot(shuffle[...], pieces[...].reshape(W, 2 * W)).astype(BF)
    for j in range(16):
        out[j] = y[j * 16 : j * 16 + 16]


def gather(call, shuffle, pieces, n):
    return call(
        gather_kernel, "gather_frequencies", (n,),
        [pl.BlockSpec((W, W), lambda t: (0, 0)), pl.BlockSpec((8 // n, 2, n, 16, 2 * W), lambda t: (t, 0, 0, 0, 0))],
        pl.BlockSpec((16, 16, 2 * W), lambda t: (0, t, 0)),
        jax.ShapeDtypeStruct((16, 16 * n, 2 * W), BF), flops=n * 1e8, nbytes=n * 500e3,
    )(shuffle, pieces)


def target_kernel(chunks, t_map, *refs):
    parts, out = refs[:chunks], refs[chunks]
    for j in range(2):
        y = dot(t_map[...], jnp.concatenate([p[j] for p in parts], axis=0))
        for c in range(2):
            for half in range(2):
                at = c * W + half * 128
                out[:, j * 4 + half * 2 + c, :] = y[:, at : at + 128]


def target(call, t_map, parts):
    return call(
        functools.partial(target_kernel, len(parts)), "target_map", (8,),
        [pl.BlockSpec((W, W), lambda t: (0, 0))]
        + [pl.BlockSpec((2, p.shape[1], 2 * W), lambda t: (t, 0, 0)) for p in parts],
        pl.BlockSpec((W, 8, 128), lambda t: (0, t, 0)),
        jax.ShapeDtypeStruct((W, 64, 128), F32), flops=1e9, nbytes=12 << 20,
    )(t_map, *parts)


def swap(value, axis, mask):
    return lax.ppermute(value, axis, [(i, i ^ mask) for i in range(lax.axis_size(axis))])


def shuffles():
    first_rows = np.zeros((W, W), np.float32)
    last_rows = np.zeros((W, W), np.float32)
    for j in range(64):
        for half in range(2):
            for c in range(2):
                first_rows[(c * 2 + half) * 64 + j, j * 4 + half * 2 + c] = 1
    for j in range(16):
        for f in range(16):
            last_rows[j * 16 + f, f * 16 + j] = 1
    return jnp.asarray(first_rows, BF), jnp.asarray(last_rows, BF)


def on_device(coeffs, angles, interp, pattern, target_map):
    src = lax.axis_index("src")
    bits = [src >> k & 1 for k in range(LEVELS)]
    h = bits[1] ^ bits[2]
    meta = jnp.stack([*bits, h]).astype(jnp.int32)
    spread, close = shuffles()
    coeffs = coeffs.reshape(2, 16, SB, 2, 2, 128).transpose(0, 1, 2, 4, 3, 5).reshape(2, 16, 4 * SB, 128)
    angles = angles.reshape(LEVELS, 2, 16, SB, W)

    offs = np.cumsum((0,) + CHUNKS)[:-1].tolist()
    order = np.concatenate(
        [
            np.asarray([m << 5 | half << 4 | off + i for m in range(8) for half in range(2) for i in range(n)])
            for off, n in zip(offs, CHUNKS)
        ]
    )
    chosen = jnp.asarray(order, jnp.int32) ^ (h << 4)
    hot = (jnp.arange(W, dtype=jnp.int32)[:, None] == chosen[None, :]).astype(BF)
    t_map = jnp.dot(target_map, hot, preferred_element_type=F32).astype(BF)

    call = Order()
    state, done = {}, {}

    def step(kind, c):
        w = state.get("w")
        if kind == "W":
            state["w"] = weights(call, meta, pattern.reshape(-1), interp)
            return
        off, n = (offs[c], CHUNKS[c]) if kind != "F" else (0, 0)
        if kind == "F":
            group = FIRST[c]
            skip, ahead = offs[group[0]], c == 0
            turned = first(call, meta, spread, coeffs, angles, skip, sum(CHUNKS[k] for k in group), ahead)
            if ahead:
                state["A"] = swap(turned[1], "src", 2)
            other = swap(turned[0], "src", 1)
            for k in group:
                state["F", k] = turned[0], other, skip
        if kind == "S":
            own, other, skip = state["F", c]
            keep, send = second(call, meta, own, other, w, angles, off, skip, n)
            state["S", c] = keep, swap(send, "src", 2)
        if kind == "T":
            turned = third(call, meta, *state["S", c], w, angles, state["A"], off, n)
            state["T", c] = turned, swap(turned, "src", 6)
        if kind == "B":
            state["B", c] = swap(back(call, *state["T", c], w, n), "src", 2)
        if kind == "X":
            pieces = split(call, *state["T", c], w, state["B", c], n)
            pieces = lax.all_to_all(pieces.reshape(-1, 2 * W), "frq", 0, 0, tiled=True)
            state["X", c] = pieces.reshape(8, 2, n, 16, 2 * W)
        if kind == "G":
            state["G", c] = gather(call, close, state["X", c], n)

    for name in STEPS:
        call.last = [done[other] for other in AFTER.get(name, ())]
        call.scale = COST / 8 if name in LIGHT else COST
        step(name[0], int(name[1:]))
        done[name] = call.result
    call.last = []
    parts = [state["G", c] for c in range(len(CHUNKS))]
    out = target(call, t_map, parts)
    return out.reshape(W, 16, 2, 2, 128).transpose(0, 1, 3, 2, 4).reshape(W, 16, 2, W)


def solution(mesh):
    return jax.shard_map(
        on_device,
        mesh=mesh,
        in_specs=(P("frq", "src", None, None), P(None, "frq", "src", None), P(), P(), P()),
        out_specs=P(None, ("src", "frq"), None, None),
        check_vma=False,
    )
```
